32 devices in a mesh: blk: 16 (over z, x, core), head: 2 (over y).
Axes of the slice: x: 2, y: 2, z: 4, core: 2. Of those that a mesh axis runs over, the one named last changes fastest.
Arguments:
- query_rows: bfloat16 [8192, 1024], P('blk', 'head'), may hold values from -24 to 24
- key_rows: bfloat16 [8192, 128], P('blk'), may hold values from -9 to 9
- value_rows: bfloat16 [8192, 128], P('blk'), may hold values from -6 to 6
- grad_out: bfloat16 [8192, 1024], P('blk', 'head'), may hold values from -6 to 6
- subtree_end: int32 [8192], P('blk'), may hold values from 1 to 8192, as said below
Outputs:
- grad_queries: bfloat16 [8192, 1024], P('blk', 'head')
- grad_keys: bfloat16 [8192, 128], P(('blk', 'head'))
- grad_values: bfloat16 [8192, 128], P(('blk', 'head'))
The draws below stay inside these ranges and needn't reach their ends.
Inputs may be any that keep to these rules, and one draw needn't show every extreme that they name: Tokens are packed depth-first in trees: j < subtree_end[j], any two subtrees are nested or apart, and j is an ancestor of i or i itself exactly when j <= i < subtree_end[j]. A tree holds at most 2048 tokens, so a token's ancestors lie at most 4 blocks of 512 positions before its own block; some token has its root exactly 4 blocks before its own.
All inputs are finite; a program needn't handle non-finite values.
Results may differ from the reference program's by a relative error of at most 0.0095.
Values may be sent and summed in bfloat16 or wider, within the bound.
A program may use at most 64 MiB of HBM per device.

```python
import math
import jax
import jax.numpy as jnp
from jax import lax

HQ = 8
DH = 128
TOK_DEV = 512
WINDOW = 4
TOKENS = 8192
N_BLK = 16


def tree_layout(key):
    key = jax.random.fold_in(key, 101)
    length_key, step_key, chain_key = jax.random.split(key, 3)
    depth_limit = WINDOW * TOK_DEV
    tree_count = TOKENS // (TOK_DEV // 4) + 2
    lengths = jax.random.randint(length_key, (tree_count,), TOK_DEV // 4, WINDOW * TOK_DEV + 1)
    slot_index = jnp.arange(tree_count)
    lengths = jnp.where(slot_index == 0, TOK_DEV // 2, jnp.where(slot_index == 1, WINDOW * TOK_DEV, lengths))
    starts = jnp.cumsum(lengths) - lengths
    root_flag = jax.ops.segment_sum(jnp.ones((tree_count,), jnp.int32), starts, num_segments=TOKENS) > 0
    tree_number = jnp.cumsum(root_flag.astype(jnp.int32)) - 1
    chain_pick = (jax.random.randint(chain_key, (tree_count,), 0, 4) == 0) | (slot_index == 1)
    in_chain = chain_pick[tree_number]
    step_draw = jax.random.randint(step_key, (TOKENS,), 0, 8)
    moves = jnp.where(step_draw < 4, 1, jnp.where(step_draw == 4, 0, 4 - step_draw))
    moves = jnp.where(in_chain, 1, moves)

    def advance(depth, inputs):
        move, is_root = inputs
        depth = jnp.where(is_root, 0, jnp.clip(depth + move, 1, depth_limit - 1)).astype(jnp.int32)
        return (depth, depth)
    unused, depths = lax.scan(advance, jnp.int32(0), (moves, root_flag))
    levels = jnp.arange(depth_limit, dtype=jnp.int32)

    def close(nearest, inputs):
        depth, position = inputs
        finish = jnp.min(jnp.where(levels <= depth, nearest, TOKENS))
        nearest = jnp.where(levels == depth, position, nearest)
        return (nearest, finish)
    unused, ends = lax.scan(close, jnp.full((depth_limit,), TOKENS, jnp.int32), (depths, jnp.arange(TOKENS, dtype=jnp.int32)), reverse=True)
    return ends.astype(jnp.int32)


def draw_subtree_end(key, part):
    return tree_layout(key)


def draw_key_rows(key, part):
    folded = jax.random.fold_in(key, 7)
    key_table = jax.random.normal(folded, (TOKENS, DH), jnp.float32)
    return key_table.astype(jnp.bfloat16)


def draw_query_rows(key, part):
    folded = jax.random.fold_in(key, 9)
    query_table = jax.random.normal(folded, (TOKENS, HQ * DH), jnp.float32)
    return query_table.astype(jnp.bfloat16)


def level_of(stream_key, extent, shards, low, high):
    gain = 1.0
    for dim, shards_of in shards:
        heights = jax.random.uniform(jax.random.fold_in(jax.random.fold_in(stream_key, 6), dim), (shards_of,), jnp.float32, low / len(shards), high / len(shards))
        gain = gain * jnp.repeat(jnp.exp(heights), extent[dim] // shards_of).reshape((-1,) + (1,) * (len(extent) - 1 - dim))
    return gain


def normal_values(own_key, extent, scale, limit, pieces=(), kind=jnp.bfloat16):
    drawn = scale * jax.random.normal(own_key, extent, jnp.float32)
    if pieces:
        drawn = drawn * level_of(own_key, extent, pieces, -0.22, 0.18)
    return jnp.clip(drawn, -limit, limit).astype(kind)


def setup_inputs(seed: int = 0) -> dict:
    key_list = jax.random.split(jax.random.key(seed), 6)
    query_rows = draw_query_rows(jax.random.fold_in(key_list[5], 71), 0)
    key_rows = draw_key_rows(jax.random.fold_in(key_list[5], 71), 0)
    value_rows = normal_values(key_list[2], (TOKENS, DH), 1.0, 6.0, ((0, 16),))
    grad_out = normal_values(key_list[3], (TOKENS, HQ * DH), 1.0, 6.0, ((0, 16), (1, 2)))
    subtree_end = draw_subtree_end(jax.random.fold_in(key_list[5], 71), 0)
    return dict(query_rows=query_rows, key_rows=key_rows, value_rows=value_rows, grad_out=grad_out, subtree_end=subtree_end)


NEGATIVE = -1e+30

def reference(query_rows, key_rows, value_rows, grad_out, subtree_end):
    score_scale = 1.0 / math.sqrt(DH)
    pad_rows = WINDOW * TOK_DEV
    key_span = pad_rows + TOK_DEV
    key_padded = jnp.concatenate([jnp.zeros((pad_rows, DH), jnp.float32), key_rows.astype(jnp.float32)], axis=0)
    value_padded = jnp.concatenate([jnp.zeros((pad_rows, DH), jnp.float32), value_rows.astype(jnp.float32)], axis=0)
    end_padded = jnp.concatenate([jnp.zeros((pad_rows,), jnp.int32), subtree_end.astype(jnp.int32)], axis=0)
    grad_start = jnp.zeros((pad_rows + TOKENS, DH), jnp.float32)

    def one_block(carry, block_index):
        key_acc, value_acc = carry
        first_row = (block_index * TOK_DEV).astype(jnp.int32)
        queries = lax.dynamic_slice_in_dim(query_rows, first_row, TOK_DEV, 0).astype(jnp.float32).reshape(TOK_DEV, HQ, DH)
        grads = lax.dynamic_slice_in_dim(grad_out, first_row, TOK_DEV, 0).astype(jnp.float32).reshape(TOK_DEV, HQ, DH)
        keys_here = lax.dynamic_slice_in_dim(key_padded, first_row, key_span, 0)
        values_here = lax.dynamic_slice_in_dim(value_padded, first_row, key_span, 0)
        ends_here = lax.dynamic_slice_in_dim(end_padded, first_row, key_span, 0)
        query_pos = first_row + jnp.arange(TOK_DEV, dtype=jnp.int32)
        key_pos = first_row - pad_rows + jnp.arange(key_span, dtype=jnp.int32)
        allowed = (key_pos[None, :] <= query_pos[:, None]) & (query_pos[:, None] < ends_here[None, :])
        scores = jnp.einsum('qhe,ke->hqk', queries, keys_here) * score_scale
        scores = jnp.where(allowed[None], scores, NEGATIVE)
        row_top = lax.optimization_barrier(jnp.max(scores, axis=-1, keepdims=True))
        row_sum = lax.optimization_barrier(jnp.sum(jnp.where(allowed[None], jnp.exp(scores - row_top), 0.0), axis=-1, keepdims=True))
        log_total = row_top + jnp.log(row_sum)
        probs = jnp.where(allowed[None], jnp.exp(scores - log_total), 0.0)
        probs_low = lax.optimization_barrier(probs.astype(jnp.bfloat16)).astype(jnp.float32)
        attended = jnp.einsum('hqk,ke->qhe', probs_low, values_here)
        out_low = lax.optimization_barrier(attended.astype(jnp.bfloat16)).astype(jnp.float32)
        delta = lax.optimization_barrier(jnp.sum(grads * out_low, axis=-1))
        prob_grad = jnp.einsum('qhe,ke->hqk', grads, values_here)
        score_grad = probs * (prob_grad - delta.T[:, :, None]) * score_scale
        score_grad = lax.optimization_barrier(score_grad.astype(jnp.bfloat16)).astype(jnp.float32)
        query_grad = jnp.einsum('hqk,ke->qhe', score_grad, keys_here).reshape(TOK_DEV, HQ * DH).astype(jnp.bfloat16)
        key_grad = jnp.einsum('hqk,qhe->ke', score_grad, queries)
        value_grad = jnp.einsum('hqk,qhe->ke', probs_low, grads)
        key_acc = lax.dynamic_update_slice_in_dim(key_acc, lax.dynamic_slice_in_dim(key_acc, first_row, key_span, 0) + key_grad, first_row, 0)
        value_acc = lax.dynamic_update_slice_in_dim(value_acc, lax.dynamic_slice_in_dim(value_acc, first_row, key_span, 0) + value_grad, first_row, 0)
        return ((key_acc, value_acc), query_grad)
    (key_acc, value_acc), query_blocks = lax.scan(one_block, (grad_start, grad_start), jnp.arange(N_BLK, dtype=jnp.int32))
    grad_queries = query_blocks.reshape(TOKENS, HQ * DH)
    grad_keys = key_acc[pad_rows:].astype(jnp.bfloat16)
    grad_values = value_acc[pad_rows:].astype(jnp.bfloat16)
    return (grad_queries, grad_keys, grad_values)
```

```python
import functools
import math

import jax
import jax.numpy as jnp
from jax import lax
from jax.experimental import pallas as pl
from jax.experimental.pallas import tpu as pltpu
from jax.sharding import PartitionSpec as P

WINDOW = 4
NEGATIVE = -1e30
CHUNK = 256
NT = (((1,), (1,)), ((), ()))
NN = (((1,), (0,)), ((), ()))
TN = (((0,), (0,)), ((), ()))


def dot(a, b, dims):
    return lax.dot_general(a, b, dims, preferred_element_type=jnp.float32)


def stats_step(d, r, q0, first, tok, heads, dim, slope, q_ref, g_ref, kv_ref, ends_ref, e_ref, dp_ref, m_ref, l_ref, t_ref, mc_ref):
    blk = lax.axis_index("blk")
    qn = tok - q0
    row0 = r * CHUNK
    rows = pl.ds(row0, CHUNK) if isinstance(r, int) else pl.ds(pl.multiple_of(row0, CHUNK), CHUNK)
    base = d * tok + row0
    slab = pl.ds(base, CHUNK) if isinstance(r, int) else pl.ds(pl.multiple_of(base, CHUNK), CHUNK)
    keys = kv_ref[d, rows, 0:dim]
    values = kv_ref[d, rows, dim : 2 * dim]
    per = CHUNK // 128
    tiles = []
    for piece in range(per):
        line = ends_ref[d, pl.ds(r * per + piece, 1), :]
        tiles.append(jnp.broadcast_to(line, (128, 128)).T)
    ends = jnp.concatenate(tiles, axis=0)
    ends = jnp.where(blk >= d, ends - blk * tok, 0)
    spot = lax.broadcasted_iota(jnp.int32, (CHUNK, 128), 1) + q0
    key_spot = lax.broadcasted_iota(jnp.int32, (CHUNK, 128), 0) + (row0 - d * tok)
    bias = []
    for piece in range(qn // 128):
        here = spot + piece * 128
        ok = here < ends
        if d == 0:
            ok = ok & (key_spot <= here)
        bias.append(jnp.where(ok, 0.0, NEGATIVE))
    bias = jnp.concatenate(bias, axis=1)
    index = d * (tok // CHUNK) + r
    for h in range(heads):
        lanes = slice(h * dim, (h + 1) * dim)
        s = dot(keys, q_ref[q0:tok, lanes], NT) + bias
        dp = dot(values, g_ref[q0:tok, lanes], NT)
        top = jnp.max(s, axis=0, keepdims=True)
        if first:
            new = top
        else:
            old = m_ref[h : h + 1, q0:tok]
            new = jnp.maximum(old, top)
        e = jnp.exp2((s - new) * slope)
        total = jnp.sum(e, axis=0, keepdims=True)
        cross = jnp.sum(e * dp, axis=0, keepdims=True)
        if not first:
            fade = jnp.exp2((old - new) * slope)
            total = total + l_ref[h : h + 1, q0:tok] * fade
            cross = cross + t_ref[h : h + 1, q0:tok] * fade
        m_ref[h : h + 1, q0:tok] = new
        l_ref[h : h + 1, q0:tok] = total
        t_ref[h : h + 1, q0:tok] = cross
        mc_ref[index, h : h + 1, q0:tok] = new
        e_ref[slab, h * tok + q0 : (h + 1) * tok] = e.astype(jnp.bfloat16)
        dp_ref[slab, h * tok + q0 : (h + 1) * tok] = dp.astype(jnp.bfloat16)


def grads_step(d, r, q0, tok, heads, dim, slope, scale, q_ref, g_ref, kv_ref, e_ref, dp_ref, m_ref, l_ref, t_ref, mc_ref, dq_ref):
    row0 = r * CHUNK
    rows = pl.ds(row0, CHUNK) if isinstance(r, int) else pl.ds(pl.multiple_of(row0, CHUNK), CHUNK)
    base = d * tok + row0
    slab = pl.ds(base, CHUNK) if isinstance(r, int) else pl.ds(pl.multiple_of(base, CHUNK), CHUNK)
    keys = kv_ref[d, rows, 0:dim]
    index = d * (tok // CHUNK) + r
    dk = jnp.zeros((CHUNK, dim), jnp.float32)
    dv = jnp.zeros((CHUNK, dim), jnp.float32)
    for h in range(heads):
        lanes = slice(h * dim, (h + 1) * dim)
        cols = slice(h * tok + q0, (h + 1) * tok)
        unit = jnp.exp2((mc_ref[index, h : h + 1, q0:tok] - m_ref[h : h + 1, q0:tok]) * slope) * l_ref[h : h + 1, q0:tok]
        p = e_ref[slab, cols].astype(jnp.float32) * unit
        ds = (p * (dp_ref[slab, cols].astype(jnp.float32) - t_ref[h : h + 1, q0:tok])).astype(jnp.bfloat16)
        dv = dv + dot(p.astype(jnp.bfloat16), g_ref[q0:tok, lanes], NN)
        dk = dk + dot(ds, q_ref[q0:tok, lanes], NN)
        dq_ref[h, :, q0:tok] += dot(keys, ds, TN)
    return dk * scale, dv


def kernel(tok, heads, dim, q_ref, g_ref, kv_ref, ends_ref, dq_out, term_ref, e_ref, dp_ref, m_ref, l_ref, t_ref, mc_ref, dq_ref):
    scale = 1.0 / math.sqrt(dim)
    slope = scale * math.log2(math.e)
    chunks = tok // CHUNK
    sizes = (tok, heads, dim, slope)

    def stats(d, r, q0=0, first=False):
        stats_step(d, r, q0, first, *sizes, q_ref, g_ref, kv_ref, ends_ref, e_ref, dp_ref, m_ref, l_ref, t_ref, mc_ref)

    def grads(d, r, q0=0):
        dk, dv = grads_step(d, r, q0, *sizes, scale, q_ref, g_ref, kv_ref, e_ref, dp_ref, m_ref, l_ref, t_ref, mc_ref, dq_ref)
        rows = pl.ds(r * CHUNK, CHUNK) if isinstance(r, int) else pl.ds(pl.multiple_of(r * CHUNK, CHUNK), CHUNK)
        term_ref[d, rows, 0:dim] = dk.astype(jnp.bfloat16)
        term_ref[d, rows, dim : 2 * dim] = dv.astype(jnp.bfloat16)

    for r in range(chunks):
        stats(0, r, r * CHUNK, r == 0)

    for d in range(1, WINDOW + 1):

        @pl.loop(0, chunks)
        def _(r, d=d):
            stats(d, r)

    inv = 1.0 / l_ref[...]
    l_ref[...] = inv
    t_ref[...] = t_ref[...] * inv
    dq_ref[...] = jnp.zeros_like(dq_ref)
    for d in (4, 3, 2, 1):

        @pl.loop(0, chunks)
        def _(r, d=d):
            grads(d, r)

    for r in range(chunks):
        grads(0, r, r * CHUNK)
    for h in range(heads):
        dq_out[:, h * dim : (h + 1) * dim] = (dq_ref[h] * scale).T.astype(jnp.bfloat16)


def passed_along(shard, axis, by):
    count = lax.axis_size(axis)
    pairs = [(i, i + by) for i in range(count) if 0 <= i + by < count]
    return lax.ppermute(shard, axis, pairs)


def body(query_rows, key_rows, value_rows, grad_out, subtree_end):
    tok, dim = key_rows.shape
    heads = query_rows.shape[1] // dim
    kv = jnp.concatenate([key_rows, value_rows], axis=1)
    ends = subtree_end.reshape(tok // 128, 128)
    kvs = [kv] + [passed_along(kv, "blk", d) for d in range(1, WINDOW + 1)]
    end_list = [ends] + [passed_along(ends, "blk", d) for d in range(1, WINDOW + 1)]
    window = WINDOW + 1
    chunks = tok // CHUNK
    dq, terms = pl.pallas_call(
        functools.partial(kernel, tok, heads, dim),
        out_shape=(
            jax.ShapeDtypeStruct((tok, heads * dim), jnp.bfloat16),
            jax.ShapeDtypeStruct((window, tok, 2 * dim), jnp.bfloat16),
        ),
        in_specs=[pl.BlockSpec(memory_space=pltpu.VMEM)] * 4,
        out_specs=[pl.BlockSpec(memory_space=pltpu.VMEM)] * 2,
        scratch_shapes=[
            pltpu.VMEM((window * tok, heads * tok), jnp.bfloat16),
            pltpu.VMEM((window * tok, heads * tok), jnp.bfloat16),
            pltpu.VMEM((heads, tok), jnp.float32),
            pltpu.VMEM((heads, tok), jnp.float32),
            pltpu.VMEM((heads, tok), jnp.float32),
            pltpu.VMEM((window * chunks, heads, tok), jnp.float32),
            pltpu.VMEM((heads, dim, tok), jnp.float32),
        ],
        compiler_params=pltpu.CompilerParams(vmem_limit_bytes=48 * 2**20),
    )(query_rows, grad_out, jnp.stack(kvs), jnp.stack(end_list))
    total = terms[0].astype(jnp.float32)
    for d in range(1, window):
        total = total + passed_along(terms[d], "blk", -d).astype(jnp.float32)
    half = lax.psum_scatter(total.astype(jnp.bfloat16), "head", scatter_dimension=0, tiled=True)
    return dq, half[:, :dim], half[:, dim:]


def solution(mesh):
    placed = (P("blk", "head"), P("blk", None), P("blk", None), P("blk", "head"), P("blk"))
    return jax.shard_map(
        body,
        mesh=mesh,
        in_specs=placed,
        out_specs=(P("blk", "head"), P(("blk", "head"), None), P(("blk", "head"), None)),
        check_vma=False,
    )
```

```python
import functools
import math

import jax
import jax.numpy as jnp
from jax import lax
from jax.experimental import pallas as pl
from jax.experimental.pallas import tpu as pltpu
from jax.sharding import PartitionSpec as P

WINDOW = 4
NEGATIVE = -1e30
CHUNK = 256
NT = (((1,), (1,)), ((), ()))
NN = (((1,), (0,)), ((), ()))
TN = (((0,), (0,)), ((), ()))


def dot(a, b, dims):
    return lax.dot_general(a, b, dims, preferred_element_type=jnp.float32)


def stats_step(d, r, q0, first, tok, heads, dim, slope, q_ref, g_ref, kv_ref, ends_ref, e_ref, dp_ref, m_ref, l_ref, t_ref, mc_ref):
    blk = lax.axis_index("blk")
    qn = tok - q0
    row0 = r * CHUNK
    rows = pl.ds(row0, CHUNK) if isinstance(r, int) else pl.ds(pl.multiple_of(row0, CHUNK), CHUNK)
    base = d * tok + row0
    slab = pl.ds(base, CHUNK) if isinstance(r, int) else pl.ds(pl.multiple_of(base, CHUNK), CHUNK)
    keys = kv_ref[d, rows, 0:dim]
    values = kv_ref[d, rows, dim : 2 * dim]
    per = CHUNK // 128
    tiles = []
    for piece in range(per):
        line = ends_ref[d, pl.ds(r * per + piece, 1), :]
        tiles.append(jnp.broadcast_to(line, (128, 128)).T)
    ends = jnp.concatenate(tiles, axis=0)
    ends = jnp.where(blk >= d, ends - blk * tok, 0)
    spot = lax.broadcasted_iota(jnp.int32, (CHUNK, 128), 1) + q0
    key_spot = lax.broadcasted_iota(jnp.int32, (CHUNK, 128), 0) + (row0 - d * tok)
    bias = []
    for piece in range(qn // 128):
        here = spot + piece * 128
        ok = here < ends
        if d == 0:
            ok = ok & (key_spot <= here)
        bias.append(jnp.where(ok, 0.0, NEGATIVE))
    bias = jnp.concatenate(bias, axis=1)
    index = d * (tok // CHUNK) + r
    for h in range(heads):
        lanes = slice(h * dim, (h + 1) * dim)
        s = dot(keys, q_ref[q0:tok, lanes], NT) + bias
        dp = dot(values, g_ref[q0:tok, lanes], NT)
        top = jnp.max(s, axis=0, keepdims=True)
        if first:
            new = top
        else:
            old = m_ref[h : h + 1, q0:tok]
            new = jnp.maximum(old, top)
        e = jnp.exp2((s - new) * slope)
        total = jnp.sum(e, axis=0, keepdims=True)
        cross = jnp.sum(e * dp, axis=0, keepdims=True)
        if not first:
            fade = jnp.exp2((old - new) * slope)
            total = total + l_ref[h : h + 1, q0:tok] * fade
            cross = cross + t_ref[h : h + 1, q0:tok] * fade
        m_ref[h : h + 1, q0:tok] = new
        l_ref[h : h + 1, q0:tok] = total
        t_ref[h : h + 1, q0:tok] = cross
        mc_ref[index, h : h + 1, q0:tok] = new
        e_ref[slab, h * tok + q0 : (h + 1) * tok] = e.astype(jnp.bfloat16)
        dp_ref[slab, h * tok + q0 : (h + 1) * tok] = dp.astype(jnp.bfloat16)


def grads_step(d, r, q0, tok, heads, dim, slope, scale, q_ref, g_ref, kv_ref, e_ref, dp_ref, m_ref, l_ref, t_ref, mc_ref, dq_ref):
    row0 = r * CHUNK
    rows = pl.ds(row0, CHUNK) if isinstance(r, int) else pl.ds(pl.multiple_of(row0, CHUNK), CHUNK)
    base = d * tok + row0
    slab = pl.ds(base, CHUNK) if isinstance(r, int) else pl.ds(pl.multiple_of(base, CHUNK), CHUNK)
    keys = kv_ref[d, rows, 0:dim]
    index = d * (tok // CHUNK) + r
    dk = jnp.zeros((CHUNK, dim), jnp.float32)
    dv = jnp.zeros((CHUNK, dim), jnp.float32)
    for h in range(heads):
        lanes = slice(h * dim, (h + 1) * dim)
        cols = slice(h * tok + q0, (h + 1) * tok)
        unit = jnp.exp2((mc_ref[index, h : h + 1, q0:tok] - m_ref[h : h + 1, q0:tok]) * slope) * l_ref[h : h + 1, q0:tok]
        p = e_ref[slab, cols].astype(jnp.float32) * unit
        ds = (p * (dp_ref[slab, cols].astype(jnp.float32) - t_ref[h : h + 1, q0:tok])).astype(jnp.bfloat16)
        dv = dv + dot(p.astype(jnp.bfloat16), g_ref[q0:tok, lanes], NN)
        dk = dk + dot(ds, q_ref[q0:tok, lanes], NN)
        dq_ref[h, :, q0:tok] += dot(keys, ds, TN)
    return dk * scale, dv


def kernel(tok, heads, dim, q_ref, g_ref, k_ref, v_ref, own_ends_ref, dq_out, dk_out, dv_out, kv_ref, ends_ref, term_ref, sib_ref, yin_ref, home_ref, e_ref, dp_ref, m_ref, l_ref, t_ref, mc_ref, dq_ref, ends_sem, direct_sem, relay_sem, core_sem, sib_sem, swap_sem, home_sem):
    scale = 1.0 / math.sqrt(dim)
    slope = scale * math.log2(math.e)
    chunks = tok // CHUNK
    sizes = (tok, heads, dim, slope)
    b = lax.axis_index("blk")
    y = lax.axis_index("head")
    count = lax.axis_size("blk")
    core = lax.rem(b, 2)
    sibling = b + 1 - 2 * core
    mine = pl.ds(pl.multiple_of(y * CHUNK, CHUNK), CHUNK)
    other = pl.ds(pl.multiple_of((1 - y) * CHUNK, CHUNK), CHUNK)

    def at(shift):
        return lax.rem(b + shift + count, count)

    def remote(src, dst, sems, slot, to_b, to_y):
        return pltpu.make_async_remote_copy(
            src_ref=src, dst_ref=dst, send_sem=sems.at[0, slot], recv_sem=sems.at[1, slot],
            device_id=(to_b, to_y), device_id_type=pl.DeviceIdType.MESH,
        )

    def ends_copy(d):
        return remote(ends_ref.at[0], ends_ref.at[d], ends_sem, d, at(d), y)

    def direct_copy(d):
        return remote(kv_ref.at[0, mine], kv_ref.at[d, mine], direct_sem, d // 2, at(d), y)

    def relay_copy(d):
        return remote(kv_ref.at[d, mine], kv_ref.at[d, mine], relay_sem, d // 2, b, 1 - y)

    def relay_arrival(d):
        return remote(kv_ref.at[d, other], kv_ref.at[d, other], relay_sem, d // 2, b, 1 - y)

    def core_copy(slot):
        return remote(kv_ref.at[slot - 1 + 2 * core], kv_ref.at[slot], core_sem, slot, sibling, y)

    def sib_copy(d):
        return remote(term_ref.at[d], sib_ref.at[d // 2], sib_sem, d // 2, sibling, y)

    def swap_copy(d):
        return remote(term_ref.at[d, other], yin_ref.at[d // 2], swap_sem, d // 2, b, 1 - y)

    def home_copy(d):
        return remote(term_ref.at[d, mine], home_ref.at[d // 2 - 1], home_sem, d // 2 - 1, at(-d), y)

    barrier = pltpu.get_barrier_semaphore()
    for d in range(1, WINDOW + 1):
        for shift in (d, -d):
            pl.semaphore_signal(barrier, inc=1, device_id=(at(shift), y), device_id_type=pl.DeviceIdType.MESH)
    pl.semaphore_signal(barrier, inc=1, device_id=(b, 1 - y), device_id_type=pl.DeviceIdType.MESH)
    kv_ref[0, :, 0:dim] = k_ref[...]
    kv_ref[0, :, dim : 2 * dim] = v_ref[...]
    ends_ref[0] = own_ends_ref[...]
    pl.semaphore_wait(barrier, 2 * WINDOW + 1)

    def stats(d, r, q0=0, first=False):
        stats_step(d, r, q0, first, *sizes, q_ref, g_ref, kv_ref, ends_ref, e_ref, dp_ref, m_ref, l_ref, t_ref, mc_ref)

    def grads(d, r, q0=0):
        dk, dv = grads_step(d, r, q0, *sizes, scale, q_ref, g_ref, kv_ref, e_ref, dp_ref, m_ref, l_ref, t_ref, mc_ref, dq_ref)
        rows = pl.ds(r * CHUNK, CHUNK) if isinstance(r, int) else pl.ds(pl.multiple_of(r * CHUNK, CHUNK), CHUNK)
        term_ref[d, rows, 0:dim] = dk.astype(jnp.bfloat16)
        term_ref[d, rows, dim : 2 * dim] = dv.astype(jnp.bfloat16)

    def all_stats(d):
        @pl.loop(0, chunks)
        def _(r):
            stats(d, r)

    for d in (2, 4):
        direct_copy(d).start()
    for d in range(1, WINDOW + 1):
        ends_copy(d).start()

    @pl.when(core == 0)
    def _():
        core_copy(1).start()

    stats(0, 0, 0, True)
    direct_copy(2).wait_recv()
    relay_copy(2).start()
    stats(0, 1, CHUNK)
    direct_copy(4).wait_recv()
    relay_copy(4).start()
    relay_arrival(2).wait_recv()

    @pl.when(core == 0)
    def _():
        core_copy(3).start()

    @pl.when(core == 1)
    def _():
        core_copy(1).start()

    for d in range(1, WINDOW + 1):
        ends_copy(d).wait_recv()
    all_stats(2)
    relay_arrival(4).wait_recv()

    @pl.when(core == 1)
    def _():
        core_copy(3).start()

    all_stats(4)
    core_copy(1).wait_recv()
    all_stats(1)
    core_copy(3).wait_recv()
    all_stats(3)

    inv = 1.0 / l_ref[...]
    l_ref[...] = inv
    t_ref[...] = t_ref[...] * inv
    dq_ref[...] = jnp.zeros_like(dq_ref)

    def add(d, rows, part):
        total = term_ref[d, rows, :].astype(jnp.float32) + part.astype(jnp.float32)
        term_ref[d, rows, :] = total.astype(jnp.bfloat16)

    def send_home(d):
        swap_copy(d).wait_recv()
        add(d, mine, yin_ref[d // 2])
        home_copy(d).start()

    for d in (3, 1):

        @pl.loop(0, chunks)
        def _(r, d=d):
            grads(d, r)

        sib_copy(d).start()

    @pl.loop(0, chunks)
    def _(i):
        r = lax.rem(1 - y + i, 2)
        grads(4, r)
        rows = pl.ds(pl.multiple_of(r * CHUNK, CHUNK), CHUNK)

        @pl.when(core == 1)
        def _():
            @pl.when(i == 0)
            def _():
                sib_copy(3).wait_recv()

            add(4, rows, sib_ref[1, rows, :])

        @pl.when(i == 0)
        def _():
            swap_copy(4).start()

    @pl.loop(0, chunks)
    def _(i):
        r = lax.rem(1 - y + i, 2)
        grads(2, r)
        rows = pl.ds(pl.multiple_of(r * CHUNK, CHUNK), CHUNK)

        @pl.when(i == 0)
        def _():
            @pl.when(core == 1)
            def _():
                sib_copy(1).wait_recv()

            @pl.when(core == 0)
            def _():
                sib_copy(3).wait_recv()

        add(2, rows, sib_ref[1 - core, rows, :])

        @pl.when(i == 0)
        def _():
            swap_copy(2).start()
            send_home(4)

    @pl.when(y == 0)
    def _():
        grads(0, 1, CHUNK)

    @pl.when(y == 1)
    def _():
        grads(0, 0)

    @pl.when(core == 0)
    def _():
        sib_copy(1).wait_recv()
        add(0, other, sib_ref[0, other, :])

    swap_copy(0).start()
    send_home(2)

    @pl.when(y == 0)
    def _():
        grads(0, 0)

    @pl.when(y == 1)
    def _():
        grads(0, 1, CHUNK)

    @pl.when(core == 0)
    def _():
        add(0, mine, sib_ref[0, mine, :])

    for h in range(heads):
        dq_out[:, h * dim : (h + 1) * dim] = (dq_ref[h] * scale).T.astype(jnp.bfloat16)
    total = term_ref[0, mine, :].astype(jnp.float32)
    for d in (2, 4):
        home_copy(d).wait_recv()
        total = total + home_ref[d // 2 - 1].astype(jnp.float32)
    swap_copy(0).wait_recv()
    total = (total + yin_ref[0].astype(jnp.float32)).astype(jnp.bfloat16)
    dk_out[...] = total[:, 0:dim]
    dv_out[...] = total[:, dim : 2 * dim]
    for d in range(1, WINDOW + 1):
        ends_copy(d).wait_send()
    for d in (2, 4):
        direct_copy(d).wait_send()
        relay_copy(d).wait_send()
        home_copy(d).wait_send()
    for d in (1, 3):
        core_copy(d).wait_send()
        sib_copy(d).wait_send()
    for d in (0, 2, 4):
        swap_copy(d).wait_send()


def body(query_rows, key_rows, value_rows, grad_out, subtree_end):
    tok, dim = key_rows.shape
    heads = query_rows.shape[1] // dim
    ends = subtree_end.reshape(tok // 128, 128)
    window = WINDOW + 1
    chunks = tok // CHUNK
    return pl.pallas_call(
        functools.partial(kernel, tok, heads, dim),
        out_shape=(
            jax.ShapeDtypeStruct((tok, heads * dim), jnp.bfloat16),
            jax.ShapeDtypeStruct((CHUNK, dim), jnp.bfloat16),
            jax.ShapeDtypeStruct((CHUNK, dim), jnp.bfloat16),
        ),
        in_specs=[pl.BlockSpec(memory_space=pltpu.VMEM)] * 5,
        out_specs=[pl.BlockSpec(memory_space=pltpu.VMEM)] * 3,
        scratch_shapes=[
            pltpu.VMEM((window, tok, 2 * dim), jnp.bfloat16),
            pltpu.VMEM((window, tok // 128, 128), jnp.int32),
            pltpu.VMEM((window, tok, 2 * dim), jnp.bfloat16),
            pltpu.VMEM((2, tok, 2 * dim), jnp.bfloat16),
            pltpu.VMEM((3, CHUNK, 2 * dim), jnp.bfloat16),
            pltpu.VMEM((2, CHUNK, 2 * dim), jnp.bfloat16),
            pltpu.VMEM((window * tok, heads * tok), jnp.bfloat16),
            pltpu.VMEM((window * tok, heads * tok), jnp.bfloat16),
            pltpu.VMEM((heads, tok), jnp.float32),
            pltpu.VMEM((heads, tok), jnp.float32),
            pltpu.VMEM((heads, tok), jnp.float32),
            pltpu.VMEM((window * chunks, heads, tok), jnp.float32),
            pltpu.VMEM((heads, dim, tok), jnp.float32),
            pltpu.SemaphoreType.DMA((2, window)),
            pltpu.SemaphoreType.DMA((2, 3)),
            pltpu.SemaphoreType.DMA((2, 3)),
            pltpu.SemaphoreType.DMA((2, 4)),
            pltpu.SemaphoreType.DMA((2, 2)),
            pltpu.SemaphoreType.DMA((2, 3)),
            pltpu.SemaphoreType.DMA((2, 2)),
        ],
        compiler_params=pltpu.CompilerParams(
            vmem_limit_bytes=48 * 2**20, collective_id=0, has_side_effects=True
        ),
    )(query_rows, grad_out, key_rows, value_rows, ends)


def solution(mesh):
    placed = (P("blk", "head"), P("blk", None), P("blk", None), P("blk", "head"), P("blk"))
    return jax.shard_map(
        body,
        mesh=mesh,
        in_specs=placed,
        out_specs=(P("blk", "head"), P(("blk", "head"), None), P(("blk", "head"), None)),
        check_vma=False,
    )
```

```python
import functools
import math

import jax
import jax.numpy as jnp
from jax import lax
from jax.experimental import pallas as pl
from jax.experimental.pallas import tpu as pltpu
from jax.sharding import PartitionSpec as P

WINDOW = 4
NEGATIVE = -1e30
CHUNK = 256
NT = (((1,), (1,)), ((), ()))
NN = (((1,), (0,)), ((), ()))
TN = (((0,), (0,)), ((), ()))


def dot(a, b, dims):
    return lax.dot_general(a, b, dims, preferred_element_type=jnp.float32)


def stats_step(d, r, q0, first, tok, heads, dim, slope, q_ref, g_ref, kv_ref, ends_ref, e_ref, dp_ref, m_ref, l_ref, t_ref, mc_ref):
    blk = lax.axis_index("blk")
    qn = tok - q0
    row0 = r * CHUNK
    rows = pl.ds(row0, CHUNK) if isinstance(r, int) else pl.ds(pl.multiple_of(row0, CHUNK), CHUNK)
    base = d * tok + row0
    slab = pl.ds(base, CHUNK) if isinstance(r, int) else pl.ds(pl.multiple_of(base, CHUNK), CHUNK)
    keys = kv_ref[d, rows, 0:dim]
    values = kv_ref[d, rows, dim : 2 * dim]
    per = CHUNK // 128
    tiles = []
    for piece in range(per):
        line = ends_ref[d, pl.ds(r * per + piece, 1), :]
        tiles.append(jnp.broadcast_to(line, (128, 128)).T)
    ends = jnp.concatenate(tiles, axis=0)
    ends = ends - blk * tok
    spot = lax.broadcasted_iota(jnp.int32, (CHUNK, 128), 1) + q0
    key_spot = lax.broadcasted_iota(jnp.int32, (CHUNK, 128), 0) + (row0 - d * tok)
    bias = []
    for piece in range(qn // 128):
        here = spot + piece * 128
        ok = here < ends
        if d == 0:
            ok = ok & (key_spot <= here)
        bias.append(jnp.where(ok, 0.0, NEGATIVE))
    bias = jnp.concatenate(bias, axis=1)
    index = d * (tok // CHUNK) + r
    for h in range(heads):
        lanes = slice(h * dim, (h + 1) * dim)
        s = dot(keys, q_ref[q0:tok, lanes], NT) + bias
        dp = dot(values, g_ref[q0:tok, lanes], NT)
        top = jnp.max(s, axis=0, keepdims=True)
        if first:
            new = top
        else:
            old = m_ref[h : h + 1, q0:tok]
            new = jnp.maximum(old, top)
        e = jnp.exp2((s - new) * slope)
        total = jnp.sum(e, axis=0, keepdims=True)
        cross = jnp.sum(e * dp, axis=0, keepdims=True)
        if not first:
            fade = jnp.exp2((old - new) * slope)
            total = total + l_ref[h : h + 1, q0:tok] * fade
            cross = cross + t_ref[h : h + 1, q0:tok] * fade
        m_ref[h : h + 1, q0:tok] = new
        l_ref[h : h + 1, q0:tok] = total
        t_ref[h : h + 1, q0:tok] = cross
        mc_ref[index, h : h + 1, q0:tok] = new
        e_ref[slab, h * tok + q0 : (h + 1) * tok] = e.astype(jnp.bfloat16)
        dp_ref[slab, h * tok + q0 : (h + 1) * tok] = dp.astype(jnp.bfloat16)


def grads_step(d, r, q0, tok, heads, dim, slope, scale, q_ref, g_ref, kv_ref, e_ref, dp_ref, m_ref, l_ref, t_ref, mc_ref, dq_ref):
    row0 = r * CHUNK
    rows = pl.ds(row0, CHUNK) if isinstance(r, int) else pl.ds(pl.multiple_of(row0, CHUNK), CHUNK)
    base = d * tok + row0
    slab = pl.ds(base, CHUNK) if isinstance(r, int) else pl.ds(pl.multiple_of(base, CHUNK), CHUNK)
    keys = kv_ref[d, rows, 0:dim]
    index = d * (tok // CHUNK) + r
    dk = jnp.zeros((CHUNK, dim), jnp.float32)
    dv = jnp.zeros((CHUNK, dim), jnp.float32)
    for h in range(heads):
        lanes = slice(h * dim, (h + 1) * dim)
        cols = slice(h * tok + q0, (h + 1) * tok)
        unit = jnp.exp2((mc_ref[index, h : h + 1, q0:tok] - m_ref[h : h + 1, q0:tok]) * slope) * l_ref[h : h + 1, q0:tok]
        p = e_ref[slab, cols].astype(jnp.float32) * unit
        ds = (p * (dp_ref[slab, cols].astype(jnp.float32) - t_ref[h : h + 1, q0:tok])).astype(jnp.bfloat16)
        dv = dv + dot(p.astype(jnp.bfloat16), g_ref[q0:tok, lanes], NN)
        dk = dk + dot(ds, q_ref[q0:tok, lanes], NN)
        dq_ref[h, :, q0:tok] += dot(keys, ds, TN)
    return dk * scale, dv


def kernel(tok, heads, dim, q_in, g_in, k_in, v_in, ends_in, dq_out, dk_out, dv_out, q_ref, g_ref, kv_ref, ends_ref, term_ref, sib_ref, yin_ref, home_ref, e_ref, dp_ref, m_ref, l_ref, t_ref, mc_ref, dq_ref, load_sem, ends_sem, direct_sem, relay_sem, core_sem, sib_sem, swap_sem, home_sem):
    scale = 1.0 / math.sqrt(dim)
    slope = scale * math.log2(math.e)
    sizes = (tok, heads, dim, slope)
    b = lax.axis_index("blk")
    y = lax.axis_index("head")
    count = lax.axis_size("blk")
    core = lax.rem(b, 2)
    sibling = b + 1 - 2 * core
    mine = pl.ds(pl.multiple_of(y * CHUNK, CHUNK), CHUNK)
    other = pl.ds(pl.multiple_of((1 - y) * CHUNK, CHUNK), CHUNK)
    halves = (mine, other)
    numbers = (y, 1 - y)

    def at(shift):
        return lax.rem(b + shift + count, count)

    def remote(src, dst, send, recv, to_b, to_y):
        return pltpu.make_async_remote_copy(
            src_ref=src, dst_ref=dst, send_sem=send, recv_sem=recv,
            device_id=(to_b, to_y), device_id_type=pl.DeviceIdType.MESH,
        )

    def ends_copy(d):
        return remote(ends_ref.at[0], ends_ref.at[d], ends_sem.at[0, d], ends_sem.at[1, d], at(d), y)

    def direct_copy(d):
        i = d // 2
        return remote(kv_ref.at[0, mine], kv_ref.at[d, mine], direct_sem.at[0, i], direct_sem.at[1, i], at(d), y)

    def relay_copy(d, rows=mine):
        i = d // 2
        return remote(kv_ref.at[d, rows], kv_ref.at[d, rows], relay_sem.at[0, i], relay_sem.at[1, i], b, 1 - y)

    def core_copy(slot, half):
        rows = halves[half]
        return remote(
            kv_ref.at[slot - 1 + 2 * core, rows], kv_ref.at[slot, rows],
            core_sem.at[0, slot, half], core_sem.at[1, slot, half], sibling, y,
        )

    def sib_copy(d, half):
        rows = halves[half]
        i = d // 2
        return remote(term_ref.at[d, rows], sib_ref.at[i, rows], sib_sem.at[0, i, half], sib_sem.at[1, i, half], sibling, y)

    def swap_copy(d):
        i = d // 2
        return remote(term_ref.at[d, other], yin_ref.at[i], swap_sem.at[0, i], swap_sem.at[1, i], b, 1 - y)

    def home_copy(d):
        i = d // 2 - 1
        return remote(term_ref.at[d, mine], home_ref.at[i], home_sem.at[0, i], home_sem.at[1, i], at(-d), y)

    loads = [
        pltpu.make_async_copy(src, dst, load_sem.at[i])
        for i, (src, dst) in enumerate(
            [
                (k_in, kv_ref.at[0, :, pl.ds(0, dim)]),
                (v_in, kv_ref.at[0, :, pl.ds(dim, dim)]),
                (ends_in, ends_ref.at[0]),
                (q_in, q_ref),
                (g_in, g_ref),
            ]
        )
    ]
    barrier = pltpu.get_barrier_semaphore()
    for d in range(1, WINDOW + 1):
        for shift in (d, -d):
            pl.semaphore_signal(barrier, inc=1, device_id=(at(shift), y), device_id_type=pl.DeviceIdType.MESH)
    pl.semaphore_signal(barrier, inc=1, device_id=(b, 1 - y), device_id_type=pl.DeviceIdType.MESH)
    for load in loads:
        load.start()
    for load in loads[:3]:
        load.wait()
    pl.semaphore_wait(barrier, 2 * WINDOW + 1)

    def stats(d, r, q0=0, first=False):
        stats_step(d, r, q0, first, *sizes, q_ref, g_ref, kv_ref, ends_ref, e_ref, dp_ref, m_ref, l_ref, t_ref, mc_ref)

    def grads(d, r, q0=0):
        dk, dv = grads_step(d, r, q0, *sizes, scale, q_ref, g_ref, kv_ref, e_ref, dp_ref, m_ref, l_ref, t_ref, mc_ref, dq_ref)
        rows = pl.ds(r * CHUNK, CHUNK) if isinstance(r, int) else pl.ds(pl.multiple_of(r * CHUNK, CHUNK), CHUNK)
        term_ref[d, rows, 0:dim] = dk.astype(jnp.bfloat16)
        term_ref[d, rows, dim : 2 * dim] = dv.astype(jnp.bfloat16)

    def when(condition, run):
        pl.when(condition)(run)

    for d in (2, 4):
        when(b + d < count, lambda d=d: direct_copy(d).start())
    for d in range(1, WINDOW + 1):
        when(b + d < count, lambda d=d: ends_copy(d).start())

    @pl.when(core == 0)
    def _():
        core_copy(1, 0).start()
        core_copy(1, 1).start()

    def pass_on(d, half):
        if d == 2:
            when((core == 0) & (sibling >= 3), lambda: core_copy(3, half).start())
            when((core == 1) & (sibling >= 1), lambda: core_copy(1, half).start())
        else:
            when((core == 1) & (sibling >= 3), lambda: core_copy(3, half).start())

    def direct_in(d):
        @pl.when(b >= d)
        def _():
            direct_copy(d).wait_recv()
            relay_copy(d).start()
            pass_on(d, 0)

    def relay_in(d):
        @pl.when(b >= d)
        def _():
            relay_copy(d, other).wait_recv()
            pass_on(d, 1)

    def remote_stats(d, half):
        @pl.when(b >= d)
        def _():
            if half == 0:
                ends_copy(d).wait_recv()
            if d % 2:
                core_copy(d, half).wait_recv()
            stats(d, numbers[half])

    for d in (2, 4):

        @pl.when(b + d >= count)
        def _(d=d):
            home_ref[d // 2 - 1] = jnp.zeros(home_ref.shape[1:], home_ref.dtype)

    for load in loads[3:]:
        load.wait()
    stats(0, 0, 0, True)
    direct_in(2)
    stats(0, 1, CHUNK)
    direct_in(4)
    remote_stats(2, 0)
    remote_stats(4, 0)
    relay_in(2)
    remote_stats(1, 0)
    relay_in(4)
    remote_stats(3, 0)
    remote_stats(2, 1)
    remote_stats(4, 1)
    remote_stats(1, 1)
    remote_stats(3, 1)

    inv = 1.0 / l_ref[...]
    l_ref[...] = inv
    t_ref[...] = t_ref[...] * inv
    dq_ref[...] = jnp.zeros_like(dq_ref)

    def add(d, rows, part):
        total = term_ref[d, rows, :].astype(jnp.float32) + part.astype(jnp.float32)
        term_ref[d, rows, :] = total.astype(jnp.bfloat16)

    def add_sibling(d, half):
        rows = halves[half]

        def take(source):
            sib_copy(source, half).wait_recv()
            add(d, rows, sib_ref[source // 2, rows, :])

        if d == 4:
            when(core == 1, lambda: take(3))
        elif d == 2:
            when(core == 0, lambda: take(3))
            when(core == 1, lambda: take(1))
        else:
            when(core == 0, lambda: take(1))

    def own_grads(half):
        when(numbers[half] == 0, lambda: grads(0, 0))
        when(numbers[half] == 1, lambda: grads(0, 1, CHUNK))
        add_sibling(0, half)

    for half in (1, 0):
        for d in (3, 4, 1, 2):

            @pl.when(b >= d)
            def _(d=d, half=half):
                grads(d, numbers[half])
                if d % 2:
                    sib_copy(d, half).start()
                else:
                    add_sibling(d, half)
                    if half == 1:
                        swap_copy(d).start()
                    else:
                        swap_copy(d).wait_recv()
                        add(d, mine, yin_ref[d // 2])
                        home_copy(d).start()

        own_grads(half)
        if half == 1:
            swap_copy(0).start()

    for h in range(heads):
        dq_out[:, h * dim : (h + 1) * dim] = (dq_ref[h] * scale).T.astype(jnp.bfloat16)
    total = term_ref[0, mine, :].astype(jnp.float32)
    swap_copy(0).wait_recv()
    total = total + yin_ref[0].astype(jnp.float32)
    for d in (4, 2):
        when(b + d < count, lambda d=d: home_copy(d).wait_recv())
        total = total + home_ref[d // 2 - 1].astype(jnp.float32)
    total = total.astype(jnp.bfloat16)
    dk_out[...] = total[:, 0:dim]
    dv_out[...] = total[:, dim : 2 * dim]
    for d in range(1, WINDOW + 1):
        when(b + d < count, lambda d=d: ends_copy(d).wait_send())
    for d in (2, 4):
        when(b + d < count, lambda d=d: direct_copy(d).wait_send())

        @pl.when(b >= d)
        def _(d=d):
            relay_copy(d).wait_send()
            swap_copy(d).wait_send()
            home_copy(d).wait_send()

    swap_copy(0).wait_send()
    for d in (1, 3):
        for half in (0, 1):
            when(sibling >= d, lambda d=d, half=half: core_copy(d, half).wait_send())
            when(b >= d, lambda d=d, half=half: sib_copy(d, half).wait_send())


def body(query_rows, key_rows, value_rows, grad_out, subtree_end):
    tok, dim = key_rows.shape
    heads = query_rows.shape[1] // dim
    ends = subtree_end.reshape(tok // 128, 128)
    window = WINDOW + 1
    chunks = tok // CHUNK
    return pl.pallas_call(
        functools.partial(kernel, tok, heads, dim),
        out_shape=(
            jax.ShapeDtypeStruct((tok, heads * dim), jnp.bfloat16),
            jax.ShapeDtypeStruct((CHUNK, dim), jnp.bfloat16),
            jax.ShapeDtypeStruct((CHUNK, dim), jnp.bfloat16),
        ),
        in_specs=[pl.BlockSpec(memory_space=pl.ANY)] * 5,
        out_specs=[pl.BlockSpec(memory_space=pltpu.VMEM)] * 3,
        scratch_shapes=[
            pltpu.VMEM((tok, heads * dim), jnp.bfloat16),
            pltpu.VMEM((tok, heads * dim), jnp.bfloat16),
            pltpu.VMEM((window, tok, 2 * dim), jnp.bfloat16),
            pltpu.VMEM((window, tok // 128, 128), jnp.int32),
            pltpu.VMEM((window, tok, 2 * dim), jnp.bfloat16),
            pltpu.VMEM((2, tok, 2 * dim), jnp.bfloat16),
            pltpu.VMEM((3, CHUNK, 2 * dim), jnp.bfloat16),
            pltpu.VMEM((2, CHUNK, 2 * dim), jnp.bfloat16),
            pltpu.VMEM((window * tok, heads * tok), jnp.bfloat16),
            pltpu.VMEM((window * tok, heads * tok), jnp.bfloat16),
            pltpu.VMEM((heads, tok), jnp.float32),
            pltpu.VMEM((heads, tok), jnp.float32),
            pltpu.VMEM((heads, tok), jnp.float32),
            pltpu.VMEM((window * chunks, heads, tok), jnp.float32),
            pltpu.VMEM((heads, dim, tok), jnp.float32),
            pltpu.SemaphoreType.DMA((5,)),
            pltpu.SemaphoreType.DMA((2, window)),
            pltpu.SemaphoreType.DMA((2, 3)),
            pltpu.SemaphoreType.DMA((2, 3)),
            pltpu.SemaphoreType.DMA((2, 4, 2)),
            pltpu.SemaphoreType.DMA((2, 2, 2)),
            pltpu.SemaphoreType.DMA((2, 3)),
            pltpu.SemaphoreType.DMA((2, 2)),
        ],
        compiler_params=pltpu.CompilerParams(
            vmem_limit_bytes=48 * 2**20, collective_id=0, has_side_effects=True
        ),
    )(query_rows, grad_out, key_rows, value_rows, ends)


def solution(mesh):
    placed = (P("blk", "head"), P("blk", None), P("blk", None), P("blk", "head"), P("blk"))
    return jax.shard_map(
        body,
        mesh=mesh,
        in_specs=placed,
        out_specs=(P("blk", "head"), P(("blk", "head"), None), P(("blk", "head"), None)),
        check_vma=False,
    )
```
